32 devices in a mesh: member: 2 (over x), lon: 8 (over z, y), lat: 2 (over core).
Axes of the slice: x: 2, y: 2, z: 4, core: 2. Of those that a mesh axis runs over, the one named last changes fastest.
Arguments:
- forcing: float32 [4, 192, 1024], P('member', 'lat', 'lon'), parts along dimension 0, may hold values from -8 to 8
- coeffs: float32 [8, 2, 192, 1024], P(None, None, 'lat', 'lon'), may hold values from 0.02 to 0.6
- sea_mask: int32 [2, 192, 1024], P(None, 'lat', 'lon'), may hold values 0 or 1
- fold_pair: int32 [1024], replicated, may hold values from 0 to 1023, as said below
- norm_scale: float32 [2, 192, 1024], P(None, 'lat', 'lon'), may hold values from 0.5 to 2
Outputs:
- adjoint_field: float32 [4, 192, 1024], P('member', 'lat', 'lon'), parts along dimension 0
The draws below stay inside these ranges and needn't reach their ends.
There are 2 independent parts, one for each index of `member`. The reference program is written for one: setup_inputs(seed, part) draws one part's arguments, and reference() takes and returns one part's arrays. A program takes and returns all parts, laid end to end along the dimension named above; an argument that names none is the same for every part. Nothing has to cross between parts.
Inputs may be any that keep to these rules, and one draw needn't show every extreme that they name: fold_pair is the tripolar fold's mirror with staggering: fold_pair[i] = (1023 - i + o_i) mod 1024, with each column's own offset o_i of 0, 1 or 2.
All inputs are finite; a program needn't handle non-finite values. No bound on the sum of `sea_mask` on one device may be relied on, other than what follows from the above.
Results may differ from the reference program's by a relative error of at most 0.00002.
Values sent between devices are 32-bit elements; how exact they have to be, the bound alone decides.
A program may use at most 64 MiB of HBM per device.

```python
import math
import jax
import jax.numpy as jnp

K = 2
STEPS = 2
ITERS = 4
NLAT = 192
NLON = 1024


def draw_fold_pair(key, part):
    key = jax.random.fold_in(key, 5)
    offsets = jax.random.randint(key, (NLON,), 0, 3).astype(jnp.int32)
    offsets = offsets.at[0].set(0).at[NLON - 1].set(0)
    column = jnp.arange(NLON, dtype=jnp.int32)
    return ((NLON - 1 - column + offsets) % NLON).astype(jnp.int32)


def touch_ends(values, stream_key, least, largest):
    longest = values.shape.index(max(values.shape))
    spots = []
    for shift in (0, 1):
        where = [jax.random.randint(jax.random.fold_in(stream_key, axis), (), 0, length) for axis, length in enumerate(values.shape)]
        where[longest] = (where[longest] + shift) % values.shape[longest]
        spots.append(tuple(where))
    return values.at[spots[0]].set(least).at[spots[1]].set(largest)


def steps_of(own_key, shape, split, smallest, top_value):
    factor_of = 1.0
    for dim, blocks in split:
        steps = jax.random.uniform(jax.random.fold_in(jax.random.fold_in(own_key, 6), dim), (blocks,), jnp.float32, smallest / len(split), top_value / len(split))
        factor_of = factor_of * jnp.repeat(jnp.exp(steps), shape[dim] // blocks).reshape((-1,) + (1,) * (len(shape) - 1 - dim))
    return factor_of


def noise(rng, dims, scale, limit, pieces=(), held_as=jnp.bfloat16):
    array = scale * jax.random.normal(rng, dims, jnp.float32)
    if pieces:
        array = array * steps_of(rng, dims, pieces, -0.22, 0.18)
    return jnp.clip(array, -limit, limit).astype(held_as)


def setup_inputs(seed: int = 0, part: int = 0) -> dict:
    arg_keys = jax.random.split(jax.random.key(seed), 6)
    part_keys = jax.random.split(jax.random.fold_in(arg_keys[5], part), 6)
    return {
        "forcing": noise(part_keys[0], (K, NLAT, NLON), 1.0, 8.0, ((1, 2), (2, 8)), jnp.float32),
        "coeffs": jnp.clip(jnp.exp(math.log(0.6) - 3.4011974 * jax.random.uniform(arg_keys[1], (8, K, NLAT, NLON), jnp.float32) ** steps_of(arg_keys[1], (8, K, NLAT, NLON), ((2, 2), (3, 8)), -0.2, 0.2)), 0.02, 0.6),
        "sea_mask": touch_ends((jax.random.randint(arg_keys[2], (K, NLAT, NLON), 0, 4) < 3).astype(jnp.int32), jax.random.fold_in(arg_keys[2], 1), 0, 1),
        "fold_pair": draw_fold_pair(jax.random.fold_in(arg_keys[5], 71), part),
        "norm_scale": jnp.clip(jnp.exp(math.log(2.0) - 1.3862944 * jax.random.uniform(arg_keys[4], (K, NLAT, NLON), jnp.float32) ** steps_of(arg_keys[4], (K, NLAT, NLON), ((1, 2), (2, 8)), -0.2, 0.2)), 0.5, 2.0),
    }


OFFSETS = ((1, 0), (-1, 0), (0, 1), (0, -1), (1, 1), (1, -1), (-1, 1), (-1, -1))
CENTRE_VALUE = 1.05
HALF_WIDTH = 0.9


def spread_field(field, coeffs, fold_pair):
    rows = field.shape[1]
    total = jnp.zeros_like(field)
    for index_dir, (shift_lat, shift_lon) in enumerate(OFFSETS):
        product = coeffs[index_dir] * field
        padded = jnp.pad(product, ((0, 0), (1, 1), (0, 0)))
        moved = padded[:, 1 - shift_lat:1 - shift_lat + rows, :]
        total = total + jnp.roll(moved, shift_lon, axis=2)
    top_row = coeffs[0][:, -1, :] * field[:, -1, :]
    placed = jnp.zeros_like(top_row).at[:, fold_pair].add(top_row)
    return total.at[:, -1, :].add(placed)


def chebyshev(rhs, apply_op, precond):
    sigma_ratio = CENTRE_VALUE / HALF_WIDTH
    ratio_now = 1.0 / sigma_ratio
    residual = rhs
    update = precond * residual / CENTRE_VALUE
    iterate = update
    for sweep in range(ITERS):
        residual = residual - apply_op(update)
        ratio_next = 1.0 / (2.0 * sigma_ratio - ratio_now)
        update = (ratio_next * ratio_now) * update + (2.0 * ratio_next / HALF_WIDTH) * (precond * residual)
        iterate = iterate + update
        ratio_now = ratio_next
    return iterate


def reference(forcing, coeffs, sea_mask, fold_pair, norm_scale):
    sea = sea_mask.astype(forcing.dtype)
    diag_sum = coeffs[0]
    for index_dir in range(1, 8):
        diag_sum = diag_sum + coeffs[index_dir]
    precond = 1.0 / (1.0 + diag_sum)

    def apply_op(field):
        return sea * ((1.0 + diag_sum) * field - spread_field(field, coeffs, fold_pair))

    state = sea * norm_scale * forcing
    for step in range(STEPS):
        state = chebyshev(state, apply_op, precond)
    return norm_scale * state
```

```python
import functools

import jax
import jax.numpy as jnp
from jax import lax
from jax.experimental import pallas as pl
from jax.experimental.pallas import tpu as pltpu
from jax.sharding import PartitionSpec as P

STEPS = 2
ITERS = 4
DEPTH = STEPS * ITERS
LANES = 128

OFFSETS = ((1, 0), (-1, 0), (0, 1), (0, -1), (1, 1), (1, -1), (-1, 1), (-1, -1))
TURNED = tuple(OFFSETS.index((-r, -c)) for r, c in OFFSETS)
CENTRE_VALUE = 1.05
HALF_WIDTH = 0.9
MESH = pl.DeviceIdType.MESH


def flipped(tile):
    lanes = lax.broadcasted_iota(jnp.int32, tile.shape, 1)
    rows = lax.broadcasted_iota(jnp.int32, tile.shape, 0)
    tile = jnp.take_along_axis(tile, tile.shape[1] - 1 - lanes, axis=1)
    for bit in (4, 2, 1):
        up = pltpu.roll(tile, bit, 0)
        down = pltpu.roll(tile, tile.shape[0] - bit, 0)
        tile = jnp.where((rows & bit) != 0, up, down)
    return tile


def kernel(
    n_lon,
    forcing,
    coeffs,
    sea_mask,
    fold,
    norm,
    out,
    to_partner,
    to_mirror,
    north,
    south,
    ext,
    weights,
    send_sems,
    recv_sems,
):
    levels, rows, cols = forcing.shape
    fields = 10 * levels
    pm_at = 8 * levels
    z_at = 9 * levels
    lon = lax.axis_index("lon")
    lat = lax.axis_index("lat")
    east = lax.rem(lon + 1, n_lon)
    west = lax.rem(lon + n_lon - 1, n_lon)
    mirror = n_lon - 1 - lon
    is_top = lat == 1

    barrier = pltpu.get_barrier_semaphore()

    def greet(where):
        pl.semaphore_signal(barrier, inc=1, device_id=where, device_id_type=MESH)

    greet({"lon": east})
    greet({"lon": west})
    greet({"lat": 1 - lat})

    @pl.when(is_top)
    def _():
        greet({"lon": mirror})

    lane = lax.broadcasted_iota(jnp.int32, (1, cols), 1)
    offset = fold[pl.ds(lon, 1), :] - (n_lon * cols - 1 - (lon * cols + lane))
    offset = jnp.where(offset < 0, offset + n_lon * cols, offset)
    row = lax.broadcasted_iota(jnp.int32, (8, cols), 0)
    at_fold = jnp.logical_and(row == 7, is_top)
    padding = jnp.zeros((LANES - rows, cols), jnp.float32)

    def keep(index, value):
        to_partner[index] = jnp.where(is_top, value[:8], value[rows - 8 :])
        level = index % levels
        group = index // levels
        turned = TURNED[group] if group < 8 else group
        to_mirror[turned * levels + level] = flipped(value[rows - 8 :])
        whole = jnp.concatenate([value, padding], axis=0)
        ext[index, DEPTH : DEPTH + cols, :] = whole.T

    for k in range(levels):
        diag_sum = coeffs[0, k]
        for d in range(1, 8):
            diag_sum = diag_sum + coeffs[d, k]
        sea = sea_mask[k].astype(jnp.float32)
        keep(pm_at + k, sea * (1.0 / (1.0 + diag_sum)))
        keep(z_at + k, sea * norm[k] * forcing[k])
        north_edge = coeffs[0, k, rows - 8 :, :]
        for d, (shift_lat, shift_lon) in enumerate(OFFSETS):
            value = coeffs[d, k]
            if shift_lat == 1:
                split = jnp.where(offset == 1 - shift_lon, north_edge, 0.0)
                edge = jnp.where(at_fold, split, value[rows - 8 :])
                value = jnp.concatenate([value[: rows - 8], edge], axis=0)
            keep(d * levels + k, value)

    def remote(source, target, which, where):
        return pltpu.make_async_remote_copy(
            src_ref=source,
            dst_ref=target,
            send_sem=send_sems.at[which],
            recv_sem=recv_sems.at[which],
            device_id=where,
            device_id_type=MESH,
        )

    down = remote(to_partner, north, 0, {"lat": 1 - lat})
    across = remote(to_mirror, north, 1, {"lon": mirror})
    up = remote(to_partner, south, 2, {"lat": 1 - lat})

    @pl.when(is_top)
    def _():
        pl.semaphore_wait(barrier, 4)
        across.start()
        down.start()

    @pl.when(jnp.logical_not(is_top))
    def _():
        pl.semaphore_wait(barrier, 3)
        up.start()
        south[...] = jnp.zeros_like(south)

    @pl.when(is_top)
    def _():
        up.wait_recv()
        across.wait_recv()

    @pl.when(jnp.logical_not(is_top))
    def _():
        down.wait_recv()

    nothing = jnp.zeros((8, cols), jnp.float32)
    for index in range(fields):
        plain = north[index]
        halo = jnp.concatenate(
            [
                jnp.where(is_top, pltpu.roll(plain, 1, 1), plain),
                jnp.where(is_top, plain, 0.0),
                nothing,
                south[index],
            ],
            axis=0,
        )
        ext[index, DEPTH : DEPTH + cols, rows : rows + 32] = halo.T

    total = cols + 2 * DEPTH
    go_west = remote(
        ext.at[:, pl.ds(DEPTH, DEPTH)], ext.at[:, pl.ds(DEPTH + cols, DEPTH)], 3, {"lon": west}
    )
    go_east = remote(ext.at[:, pl.ds(cols, DEPTH)], ext.at[:, pl.ds(0, DEPTH)], 4, {"lon": east})
    go_west.start()
    go_east.start()
    go_west.wait()
    go_east.wait()

    lane_row = lax.broadcasted_iota(jnp.int32, (fields, LANES), 1)
    ghost = jnp.logical_and(jnp.logical_and(lane_row >= rows, lane_row < rows + 8), is_top)
    for seam in (DEPTH, DEPTH + cols):
        before = pltpu.roll(ext[:, seam - 1, :], LANES - 8, 1)
        ext[:, seam, :] = jnp.where(ghost, before, ext[:, seam, :])

    lane_all = lax.broadcasted_iota(jnp.int32, (total, LANES), 1)
    inside = jnp.logical_or(lane_all < rows + 8, lane_all >= LANES - 8)

    def turn(value, shift, axis):
        shift = shift % value.shape[axis]
        return value if shift == 0 else pltpu.roll(value, shift, axis)

    scale = []
    for k in range(levels):
        pm = jnp.where(inside, ext[pm_at + k], 0.0)
        ext[pm_at + k] = pm
        pm_by = {c: turn(pm, -c, 0) for c in (-1, 0, 1)}
        for d, (shift_lat, shift_lon) in enumerate(OFFSETS):
            source = turn(ext[d * levels + k], shift_lat, 1)
            weights[d * levels + k] = pm_by[shift_lon] * source

    def spread(u, k):
        by_lat = {r: turn(u, r, 1) for r in (-1, 0, 1)}
        groups = {}
        for d, (shift_lat, shift_lon) in enumerate(OFFSETS):
            term = weights[d * levels + k] * by_lat[shift_lat]
            groups[shift_lon] = groups[shift_lon] + term if shift_lon in groups else term
        return groups[0] + turn(groups[1], 1, 0) + turn(groups[-1], -1, 0)

    sigma_ratio = CENTRE_VALUE / HALF_WIDTH
    state = [ext[z_at + k] for k in range(levels)]
    for step in range(STEPS):
        ratio_now = 1.0 / sigma_ratio
        scaled = [ext[pm_at + k] * state[k] for k in range(levels)]
        update = [value * (1.0 / CENTRE_VALUE) for value in scaled]
        state = list(update)
        for sweep in range(ITERS):
            ratio_next = 1.0 / (2.0 * sigma_ratio - ratio_now)
            for k in range(levels):
                scaled[k] = scaled[k] - update[k] + spread(update[k], k)
                update[k] = (ratio_next * ratio_now) * update[k] + (
                    2.0 * ratio_next / HALF_WIDTH
                ) * scaled[k]
                state[k] = state[k] + update[k]
            ratio_now = ratio_next

    for k in range(levels):
        own = state[k][DEPTH : DEPTH + cols].T
        out[k] = norm[k] * own[:rows]

    @pl.when(is_top)
    def _():
        down.wait_send()
        across.wait_send()

    @pl.when(jnp.logical_not(is_top))
    def _():
        up.wait_send()


def body(n_lon, forcing, coeffs, sea_mask, fold_pair, norm_scale):
    levels, rows, cols = forcing.shape
    fields = 10 * levels
    edge = pltpu.VMEM((fields, 8, cols), jnp.float32)
    return pl.pallas_call(
        functools.partial(kernel, n_lon),
        out_shape=jax.ShapeDtypeStruct(forcing.shape, jnp.float32),
        in_specs=[pl.BlockSpec(memory_space=pltpu.VMEM)] * 5,
        out_specs=pl.BlockSpec(memory_space=pltpu.VMEM),
        scratch_shapes=[
            edge,
            edge,
            edge,
            edge,
            pltpu.VMEM((fields, cols + 2 * DEPTH, LANES), jnp.float32),
            pltpu.VMEM((8 * levels, cols + 2 * DEPTH, LANES), jnp.float32),
            pltpu.SemaphoreType.DMA((5,)),
            pltpu.SemaphoreType.DMA((5,)),
        ],
        compiler_params=pltpu.CompilerParams(
            collective_id=0, has_side_effects=True, vmem_limit_bytes=32 * 1024 * 1024
        ),
    )(forcing, coeffs, sea_mask, fold_pair.reshape(n_lon, cols), norm_scale)


def solution(mesh):
    placed = (
        P("member", "lat", "lon"),
        P(None, None, "lat", "lon"),
        P(None, "lat", "lon"),
        P(),
        P(None, "lat", "lon"),
    )
    return jax.shard_map(
        functools.partial(body, mesh.shape["lon"]),
        mesh=mesh,
        in_specs=placed,
        out_specs=P("member", "lat", "lon"),
        check_vma=False,
    )
```

```python
import functools

import jax
import jax.numpy as jnp
from jax import lax
from jax.experimental import pallas as pl
from jax.experimental.pallas import tpu as pltpu
from jax.sharding import PartitionSpec as P

STEPS = 2
ITERS = 4
DEPTH = STEPS * ITERS
LANES = 128

OFFSETS = ((1, 0), (-1, 0), (0, 1), (0, -1), (1, 1), (1, -1), (-1, 1), (-1, -1))
TURNED = tuple(OFFSETS.index((-r, -c)) for r, c in OFFSETS)
CENTRE_VALUE = 1.05
HALF_WIDTH = 0.9
MESH = pl.DeviceIdType.MESH


def flipped(tile):
    lanes = lax.broadcasted_iota(jnp.int32, tile.shape, 1)
    rows = lax.broadcasted_iota(jnp.int32, tile.shape, 0)
    tile = jnp.take_along_axis(tile, tile.shape[1] - 1 - lanes, axis=1)
    for bit in (4, 2, 1):
        up = pltpu.roll(tile, bit, 0)
        down = pltpu.roll(tile, tile.shape[0] - bit, 0)
        tile = jnp.where((rows & bit) != 0, up, down)
    return tile


def kernel(
    n_lon,
    forcing_hbm,
    coeffs_hbm,
    mask_hbm,
    fold_hbm,
    norm_hbm,
    out,
    forcing,
    coeffs,
    sea_mask,
    fold,
    norm,
    to_partner,
    to_mirror,
    north,
    south,
    ext,
    weights,
    update,
    residual,
    iterate,
    load_sems,
    send_sems,
    recv_sems,
):
    levels, rows, cols = forcing.shape
    fields = 10 * levels
    pm_at = 8 * levels
    z_at = 9 * levels
    total = cols + 2 * DEPTH
    lon = lax.axis_index("lon")
    lat = lax.axis_index("lat")
    east = lax.rem(lon + 1, n_lon)
    west = lax.rem(lon + n_lon - 1, n_lon)
    mirror = n_lon - 1 - lon
    is_top = lat == 1

    loads = [
        pltpu.make_async_copy(source, target, load_sems.at[i])
        for i, (source, target) in enumerate(
            (
                (coeffs_hbm, coeffs),
                (forcing_hbm, forcing),
                (mask_hbm, sea_mask),
                (norm_hbm, norm),
                (fold_hbm, fold),
            )
        )
    ]
    for load in loads:
        load.start()

    barrier = pltpu.get_barrier_semaphore()

    def greet(where):
        pl.semaphore_signal(barrier, inc=1, device_id=where, device_id_type=MESH)

    greet({"lon": east})
    greet({"lon": west})
    greet({"lat": 1 - lat})

    @pl.when(is_top)
    def _():
        greet({"lon": mirror})

    for load in loads:
        load.wait()

    lane = lax.broadcasted_iota(jnp.int32, (1, cols), 1)
    offset = fold[pl.ds(lon, 1), :] - (n_lon * cols - 1 - (lon * cols + lane))
    offset = jnp.where(offset < 0, offset + n_lon * cols, offset)
    sub = lax.broadcasted_iota(jnp.int32, (8, cols), 0)
    at_fold = jnp.logical_and(sub == 7, is_top)

    def fields_of(k, start, stop):
        c = [coeffs[d, k, start:stop, :] for d in range(8)]
        diag_sum = c[0]
        for d in range(1, 8):
            diag_sum = diag_sum + c[d]
        sea = sea_mask[k, start:stop, :].astype(jnp.float32)
        pm = sea * (1.0 / (1.0 + diag_sum))
        if stop == rows:
            cut = rows - 8 - start
            north_edge = c[0][cut:]
            for d, (shift_lat, shift_lon) in enumerate(OFFSETS):
                if shift_lat == 1:
                    split = jnp.where(offset == 1 - shift_lon, north_edge, 0.0)
                    edge = jnp.where(at_fold, split, c[d][cut:])
                    c[d] = jnp.concatenate([c[d][:cut], edge], axis=0) if cut else edge
        z = sea * norm[k, start:stop, :] * forcing[k, start:stop, :]
        return [value * pm for value in c] + [pm, z]

    for k in range(levels):
        top = fields_of(k, rows - 8, rows)
        bottom = fields_of(k, 0, 8)
        for group in range(10):
            to_partner[group * levels + k] = jnp.where(is_top, bottom[group], top[group])
            turned = TURNED[group] if group < 8 else group
            to_mirror[turned * levels + k] = flipped(top[group])

    def remote(source, target, which, where):
        return pltpu.make_async_remote_copy(
            src_ref=source,
            dst_ref=target,
            send_sem=send_sems.at[which],
            recv_sem=recv_sems.at[which],
            device_id=where,
            device_id_type=MESH,
        )

    down = remote(to_partner, north, 0, {"lat": 1 - lat})
    across = remote(to_mirror, north, 1, {"lon": mirror})
    up = remote(to_partner, south, 2, {"lat": 1 - lat})

    @pl.when(is_top)
    def _():
        pl.semaphore_wait(barrier, 4)
        across.start()
        down.start()

    @pl.when(jnp.logical_not(is_top))
    def _():
        pl.semaphore_wait(barrier, 3)
        up.start()
        south[...] = jnp.zeros_like(south)

    padding = jnp.zeros((LANES - rows, cols), jnp.float32)
    for k in range(levels):
        for group, value in enumerate(fields_of(k, 0, rows)):
            whole = jnp.concatenate([value, padding], axis=0)
            ext[group * levels + k, DEPTH : DEPTH + cols, :] = whole.T

    @pl.when(is_top)
    def _():
        up.wait_recv()
        across.wait_recv()

    @pl.when(jnp.logical_not(is_top))
    def _():
        down.wait_recv()

    nothing = jnp.zeros((8, cols), jnp.float32)
    for first in range(0, fields, 4):
        several = range(first, min(first + 4, fields))
        halo = []
        for index in several:
            plain = north[index]
            halo += [
                jnp.where(is_top, pltpu.roll(plain, 1, 1), plain),
                jnp.where(is_top, plain, 0.0),
                nothing,
                south[index],
            ]
        halo = jnp.concatenate(halo, axis=0).T
        for i, index in enumerate(several):
            ext[index, DEPTH : DEPTH + cols, LANES - 32 :] = halo[:, 32 * i : 32 * i + 32]

    go_west = remote(
        ext.at[:, pl.ds(DEPTH, DEPTH)], ext.at[:, pl.ds(DEPTH + cols, DEPTH)], 3, {"lon": west}
    )
    go_east = remote(ext.at[:, pl.ds(cols, DEPTH)], ext.at[:, pl.ds(0, DEPTH)], 4, {"lon": east})
    go_west.start()
    go_east.start()

    def place(start, stop):
        lanes = lax.broadcasted_iota(jnp.int32, (stop - start, LANES), 1)
        inside = jnp.logical_or(lanes < rows + 8, lanes >= LANES - 8)
        for k in range(levels):
            for d, (shift_lat, _) in enumerate(OFFSETS):
                value = jnp.where(inside, ext[d * levels + k, start:stop, :], 0.0)
                if shift_lat:
                    value = pltpu.roll(value, shift_lat % LANES, 1)
                weights[d * levels + k, start:stop, :] = value

    place(2 * DEPTH, DEPTH + cols)
    go_west.wait()
    go_east.wait()

    lane_row = lax.broadcasted_iota(jnp.int32, (fields, LANES), 1)
    ghost = jnp.logical_and(jnp.logical_and(lane_row >= rows, lane_row < rows + 8), is_top)
    for seam in (DEPTH, DEPTH + cols):
        before = pltpu.roll(ext[:, seam - 1, :], LANES - 8, 1)
        ext[:, seam, :] = jnp.where(ghost, before, ext[:, seam, :])
    place(0, 2 * DEPTH)
    place(DEPTH + cols, total)

    chunks = total // 8
    sub_all = lax.broadcasted_iota(jnp.int32, (8, LANES), 0)
    low, high = sub_all == 0, sub_all == 7

    def parts(k, s):
        at = pl.ds(8 * s, 8)
        u = update[k, at, :]
        by_lat = {0: u, 1: pltpu.roll(u, 1, 1), -1: pltpu.roll(u, LANES - 1, 1)}
        sums = {}
        for d, (shift_lat, shift_lon) in enumerate(OFFSETS):
            term = weights[d * levels + k, at, :] * by_lat[shift_lat]
            sums[shift_lon] = sums[shift_lon] + term if shift_lon in sums else term
        return sums[-1], sums[0], sums[1], u

    def sweep(keep_ratio, gain):
        held = [[None] * chunks for _ in range(levels)]
        for s in range(chunks + 1):
            for k in range(levels):
                if s < chunks:
                    held[k][s] = parts(k, s)
                if s == 0:
                    continue
                t = s - 1
                here = held[k][t]
                left = held[k][t - 1][2] if t else here[2]
                right = held[k][s][0] if s < chunks else here[0]
                gained = (
                    here[1]
                    + pltpu.roll(jnp.where(high, left, here[2]), 1, 0)
                    + pltpu.roll(jnp.where(low, right, here[0]), 7, 0)
                )
                at = pl.ds(8 * t, 8)
                res = (residual[k, at, :] - here[3]) + gained
                new = keep_ratio * here[3] + gain * res
                residual[k, at, :] = res
                update[k, at, :] = new
                iterate[k, at, :] = iterate[k, at, :] + new

    sigma_ratio = CENTRE_VALUE / HALF_WIDTH
    ratio_now = 1.0 / sigma_ratio
    factors = []
    for _ in range(ITERS):
        ratio_next = 1.0 / (2.0 * sigma_ratio - ratio_now)
        factors.append((ratio_next * ratio_now, 2.0 * ratio_next / HALF_WIDTH))
        ratio_now = ratio_next

    def pick(values, i):
        chosen = jnp.float32(values[-1])
        for n in range(len(values) - 1):
            chosen = jnp.where(i == n, jnp.float32(values[n]), chosen)
        return chosen

    for step in range(STEPS):
        for k in range(levels):
            start = ext[z_at + k] if step == 0 else ext[pm_at + k] * iterate[k]
            residual[k] = start
            first = start * (1.0 / CENTRE_VALUE)
            update[k] = first
            iterate[k] = first

        @pl.loop(0, ITERS)
        def _(i):
            sweep(pick([f[0] for f in factors], i), pick([f[1] for f in factors], i))

    for k in range(levels):
        own = (ext[pm_at + k, DEPTH : DEPTH + cols] * iterate[k, DEPTH : DEPTH + cols]).T
        out[k] = norm[k] * own[:rows]

    @pl.when(is_top)
    def _():
        down.wait_send()
        across.wait_send()

    @pl.when(jnp.logical_not(is_top))
    def _():
        up.wait_send()


def body(n_lon, forcing, coeffs, sea_mask, fold_pair, norm_scale):
    levels, rows, cols = forcing.shape
    fields = 10 * levels
    total = cols + 2 * DEPTH
    edge = pltpu.VMEM((fields, 8, cols), jnp.float32)
    tile = pltpu.VMEM(forcing.shape, jnp.float32)
    field = pltpu.VMEM((levels, total, LANES), jnp.float32)
    return pl.pallas_call(
        functools.partial(kernel, n_lon),
        out_shape=jax.ShapeDtypeStruct(forcing.shape, jnp.float32),
        in_specs=[pl.BlockSpec(memory_space=pltpu.HBM)] * 5,
        out_specs=pl.BlockSpec(memory_space=pltpu.VMEM),
        scratch_shapes=[
            tile,
            pltpu.VMEM(coeffs.shape, jnp.float32),
            pltpu.VMEM(sea_mask.shape, jnp.int32),
            pltpu.VMEM((n_lon, cols), jnp.int32),
            tile,
            edge,
            edge,
            edge,
            edge,
            pltpu.VMEM((fields, total, LANES), jnp.float32),
            pltpu.VMEM((8 * levels, total, LANES), jnp.float32),
            field,
            field,
            field,
            pltpu.SemaphoreType.DMA((5,)),
            pltpu.SemaphoreType.DMA((5,)),
            pltpu.SemaphoreType.DMA((5,)),
        ],
        compiler_params=pltpu.CompilerParams(
            collective_id=0, has_side_effects=True, vmem_limit_bytes=32 * 1024 * 1024
        ),
    )(forcing, coeffs, sea_mask, fold_pair.reshape(n_lon, cols), norm_scale)


def solution(mesh):
    placed = (
        P("member", "lat", "lon"),
        P(None, None, "lat", "lon"),
        P(None, "lat", "lon"),
        P(),
        P(None, "lat", "lon"),
    )
    return jax.shard_map(
        functools.partial(body, mesh.shape["lon"]),
        mesh=mesh,
        in_specs=placed,
        out_specs=P("member", "lat", "lon"),
        check_vma=False,
    )
```

```python
import functools

import jax
import jax.numpy as jnp
from jax import lax
from jax.experimental import pallas as pl
from jax.experimental.pallas import tpu as pltpu
from jax.sharding import PartitionSpec as P

STEPS = 2
ITERS = 4
DEPTH = STEPS * ITERS
LANES = 128

OFFSETS = ((1, 0), (-1, 0), (0, 1), (0, -1), (1, 1), (1, -1), (-1, 1), (-1, -1))
TURNED = tuple(OFFSETS.index((-r, -c)) for r, c in OFFSETS)
CENTRE_VALUE = 1.05
HALF_WIDTH = 0.9
MESH = pl.DeviceIdType.MESH


def flipped(tile):
    lanes = lax.broadcasted_iota(jnp.int32, tile.shape, 1)
    rows = lax.broadcasted_iota(jnp.int32, tile.shape, 0)
    tile = jnp.take_along_axis(tile, tile.shape[1] - 1 - lanes, axis=1)
    for bit in (4, 2, 1):
        up = pltpu.roll(tile, bit, 0)
        down = pltpu.roll(tile, tile.shape[0] - bit, 0)
        tile = jnp.where((rows & bit) != 0, up, down)
    return tile


def kernel(
    n_lon,
    forcing_hbm,
    coeffs_hbm,
    mask_hbm,
    fold_hbm,
    norm_hbm,
    out,
    forcing,
    coeffs,
    sea_mask,
    fold,
    norm,
    to_partner,
    to_mirror,
    north,
    south,
    ext,
    weights,
    update,
    residual,
    iterate,
    load_sems,
    send_sems,
    recv_sems,
):
    levels, rows, cols = forcing.shape
    fields = 10 * levels
    pm_at = 8 * levels
    z_at = 9 * levels
    total = cols + 2 * DEPTH
    lon = lax.axis_index("lon")
    lat = lax.axis_index("lat")
    east = lax.rem(lon + 1, n_lon)
    west = lax.rem(lon + n_lon - 1, n_lon)
    mirror = n_lon - 1 - lon
    is_top = lat == 1

    loads = [
        pltpu.make_async_copy(source, target, load_sems.at[i])
        for i, (source, target) in enumerate(
            (
                (coeffs_hbm, coeffs),
                (forcing_hbm, forcing),
                (mask_hbm, sea_mask),
                (norm_hbm, norm),
                (fold_hbm, fold),
            )
        )
    ]
    for load in loads:
        load.start()

    barrier = pltpu.get_barrier_semaphore()

    def greet(where):
        pl.semaphore_signal(barrier, inc=1, device_id=where, device_id_type=MESH)

    greet({"lon": east})
    greet({"lon": west})
    greet({"lat": 1 - lat})

    @pl.when(is_top)
    def _():
        greet({"lon": mirror})

    for load in loads:
        load.wait()

    lane = lax.broadcasted_iota(jnp.int32, (1, cols), 1)
    offset = fold[pl.ds(lon, 1), :] - (n_lon * cols - 1 - (lon * cols + lane))
    offset = jnp.where(offset < 0, offset + n_lon * cols, offset)
    sub = lax.broadcasted_iota(jnp.int32, (8, cols), 0)
    at_fold = jnp.logical_and(sub == 7, is_top)

    def fields_of(k, start, stop):
        c = [coeffs[d, k, start:stop, :] for d in range(8)]
        diag_sum = c[0]
        for d in range(1, 8):
            diag_sum = diag_sum + c[d]
        sea = sea_mask[k, start:stop, :].astype(jnp.float32)
        pm = sea * (1.0 / (1.0 + diag_sum))
        if stop == rows:
            cut = rows - 8 - start
            north_edge = c[0][cut:]
            for d, (shift_lat, shift_lon) in enumerate(OFFSETS):
                if shift_lat == 1:
                    split = jnp.where(offset == 1 - shift_lon, north_edge, 0.0)
                    edge = jnp.where(at_fold, split, c[d][cut:])
                    c[d] = jnp.concatenate([c[d][:cut], edge], axis=0) if cut else edge
        z = sea * norm[k, start:stop, :] * forcing[k, start:stop, :]
        return [value * pm for value in c] + [pm, z]

    for k in range(levels):
        top = fields_of(k, rows - 8, rows)
        bottom = fields_of(k, 0, 8)
        for group in range(10):
            to_partner[group * levels + k] = jnp.where(is_top, bottom[group], top[group])
            turned = TURNED[group] if group < 8 else group
            to_mirror[turned * levels + k] = flipped(top[group])

    def remote(source, target, which, where):
        return pltpu.make_async_remote_copy(
            src_ref=source,
            dst_ref=target,
            send_sem=send_sems.at[which],
            recv_sem=recv_sems.at[which],
            device_id=where,
            device_id_type=MESH,
        )

    down = remote(to_partner, north, 0, {"lat": 1 - lat})
    across = remote(to_mirror, north, 1, {"lon": mirror})
    up = remote(to_partner, south, 2, {"lat": 1 - lat})

    @pl.when(is_top)
    def _():
        pl.semaphore_wait(barrier, 4)
        across.start()
        down.start()

    @pl.when(jnp.logical_not(is_top))
    def _():
        pl.semaphore_wait(barrier, 3)
        up.start()
        south[...] = jnp.zeros_like(south)

    padding = jnp.zeros((LANES - rows, cols), jnp.float32)
    for k in range(levels):
        for group, value in enumerate(fields_of(k, 0, rows)):
            whole = jnp.concatenate([value, padding], axis=0)
            ext[group * levels + k, DEPTH : DEPTH + cols, :] = whole.T

    @pl.when(is_top)
    def _():
        up.wait_recv()
        across.wait_recv()

    @pl.when(jnp.logical_not(is_top))
    def _():
        down.wait_recv()

    nothing = jnp.zeros((8, cols), jnp.float32)
    for first in range(0, fields, 4):
        several = range(first, min(first + 4, fields))
        halo = []
        for index in several:
            plain = north[index]
            halo += [
                jnp.where(is_top, pltpu.roll(plain, 1, 1), plain),
                jnp.where(is_top, plain, 0.0),
                nothing,
                south[index],
            ]
        halo = jnp.concatenate(halo, axis=0).T
        for i, index in enumerate(several):
            ext[index, DEPTH : DEPTH + cols, LANES - 32 :] = halo[:, 32 * i : 32 * i + 32]

    go_west = remote(
        ext.at[:, pl.ds(DEPTH, DEPTH)], ext.at[:, pl.ds(DEPTH + cols, DEPTH)], 3, {"lon": west}
    )
    go_east = remote(ext.at[:, pl.ds(cols, DEPTH)], ext.at[:, pl.ds(0, DEPTH)], 4, {"lon": east})
    go_west.start()
    go_east.start()

    def place(start, stop):
        lanes = lax.broadcasted_iota(jnp.int32, (stop - start, LANES), 1)
        inside = jnp.logical_or(lanes < rows + 8, lanes >= LANES - 8)
        for k in range(levels):
            for d, (shift_lat, _) in enumerate(OFFSETS):
                value = jnp.where(inside, ext[d * levels + k, start:stop, :], 0.0)
                if shift_lat:
                    value = pltpu.roll(value, shift_lat % LANES, 1)
                weights[d * levels + k, start:stop, :] = value

    place(2 * DEPTH, DEPTH + cols)
    go_west.wait()
    go_east.wait()

    lane_row = lax.broadcasted_iota(jnp.int32, (fields, LANES), 1)
    ghost = jnp.logical_and(jnp.logical_and(lane_row >= rows, lane_row < rows + 8), is_top)
    for seam in (DEPTH, DEPTH + cols):
        before = pltpu.roll(ext[:, seam - 1, :], LANES - 8, 1)
        ext[:, seam, :] = jnp.where(ghost, before, ext[:, seam, :])
    place(0, 2 * DEPTH)
    place(DEPTH + cols, total)

    chunks = total // 8
    sub_all = lax.broadcasted_iota(jnp.int32, (8, LANES), 0)
    low, high = sub_all == 0, sub_all == 7

    def parts(k, s):
        at = pl.ds(8 * s, 8)
        u = update[k, at, :]
        by_lat = {0: u, 1: pltpu.roll(u, 1, 1), -1: pltpu.roll(u, LANES - 1, 1)}
        sums = {}
        for d, (shift_lat, shift_lon) in enumerate(OFFSETS):
            term = weights[d * levels + k, at, :] * by_lat[shift_lat]
            sums[shift_lon] = sums[shift_lon] + term if shift_lon in sums else term
        return sums[-1], sums[0], sums[1], u

    def sweep(keep_ratio, gain):
        held = [[None] * chunks for _ in range(levels)]
        for s in range(chunks + 1):
            for k in range(levels):
                if s < chunks:
                    held[k][s] = parts(k, s)
                if s == 0:
                    continue
                t = s - 1
                here = held[k][t]
                left = held[k][t - 1][2] if t else here[2]
                right = held[k][s][0] if s < chunks else here[0]
                gained = (
                    here[1]
                    + pltpu.roll(jnp.where(high, left, here[2]), 1, 0)
                    + pltpu.roll(jnp.where(low, right, here[0]), 7, 0)
                )
                at = pl.ds(8 * t, 8)
                res = (residual[k, at, :] - here[3]) + gained
                new = keep_ratio * here[3] + gain * res
                residual[k, at, :] = res
                update[k, at, :] = new
                iterate[k, at, :] = iterate[k, at, :] + new

    sigma_ratio = CENTRE_VALUE / HALF_WIDTH
    ratio_now = 1.0 / sigma_ratio
    factors = []
    for _ in range(ITERS):
        ratio_next = 1.0 / (2.0 * sigma_ratio - ratio_now)
        factors.append((ratio_next * ratio_now, 2.0 * ratio_next / HALF_WIDTH))
        ratio_now = ratio_next

    def pick(values, i):
        chosen = jnp.float32(values[-1])
        for n in range(len(values) - 1):
            chosen = jnp.where(i == n, jnp.float32(values[n]), chosen)
        return chosen

    for step in range(STEPS):
        for k in range(levels):
            start = ext[z_at + k] if step == 0 else ext[pm_at + k] * iterate[k]
            residual[k] = start
            first = start * (1.0 / CENTRE_VALUE)
            update[k] = first
            iterate[k] = first

        @pl.loop(0, ITERS)
        def _(i):
            sweep(pick([f[0] for f in factors], i), pick([f[1] for f in factors], i))

    for k in range(levels):
        own = (ext[pm_at + k, DEPTH : DEPTH + cols] * iterate[k, DEPTH : DEPTH + cols]).T
        out[k] = norm[k] * own[:rows]

    @pl.when(is_top)
    def _():
        down.wait_send()
        across.wait_send()

    @pl.when(jnp.logical_not(is_top))
    def _():
        up.wait_send()


def body(n_lon, forcing, coeffs, sea_mask, fold_pair, norm_scale):
    levels, rows, cols = forcing.shape
    fields = 10 * levels
    total = cols + 2 * DEPTH
    edge = pltpu.VMEM((fields, 8, cols), jnp.float32)
    tile = pltpu.VMEM(forcing.shape, jnp.float32)
    field = pltpu.VMEM((levels, total, LANES), jnp.float32)
    return pl.pallas_call(
        functools.partial(kernel, n_lon),
        out_shape=jax.ShapeDtypeStruct(forcing.shape, jnp.float32),
        in_specs=[pl.BlockSpec(memory_space=pltpu.HBM)] * 5,
        out_specs=pl.BlockSpec(memory_space=pltpu.VMEM),
        scratch_shapes=[
            tile,
            pltpu.VMEM(coeffs.shape, jnp.float32),
            pltpu.VMEM(sea_mask.shape, jnp.int32),
            pltpu.VMEM((n_lon, cols), jnp.int32),
            tile,
            edge,
            edge,
            edge,
            edge,
            pltpu.VMEM((fields, total, LANES), jnp.float32),
            pltpu.VMEM((8 * levels, total, LANES), jnp.float32),
            field,
            field,
            field,
            pltpu.SemaphoreType.DMA((5,)),
            pltpu.SemaphoreType.DMA((5,)),
            pltpu.SemaphoreType.DMA((5,)),
        ],
        compiler_params=pltpu.CompilerParams(
            collective_id=0, has_side_effects=True, vmem_limit_bytes=60 * 1024 * 1024
        ),
    )(forcing, coeffs, sea_mask, fold_pair.reshape(n_lon, cols), norm_scale)


def solution(mesh):
    placed = (
        P("member", "lat", "lon"),
        P(None, None, "lat", "lon"),
        P(None, "lat", "lon"),
        P(),
        P(None, "lat", "lon"),
    )
    return jax.shard_map(
        functools.partial(body, mesh.shape["lon"]),
        mesh=mesh,
        in_specs=placed,
        out_specs=P("member", "lat", "lon"),
        check_vma=False,
    )
```

```python
import functools

import jax
import jax.numpy as jnp
from jax import lax
from jax.experimental import pallas as pl
from jax.experimental.pallas import tpu as pltpu
from jax.sharding import PartitionSpec as P

STEPS = 2
ITERS = 4
DEPTH = STEPS * ITERS
LANES = 128

OFFSETS = ((1, 0), (-1, 0), (0, 1), (0, -1), (1, 1), (1, -1), (-1, 1), (-1, -1))
TURNED = tuple(OFFSETS.index((-r, -c)) for r, c in OFFSETS)
CENTRE_VALUE = 1.05
HALF_WIDTH = 0.9
MESH = pl.DeviceIdType.MESH


def flipped(tile):
    lanes = lax.broadcasted_iota(jnp.int32, tile.shape, 1)
    rows = lax.broadcasted_iota(jnp.int32, tile.shape, 0)
    tile = jnp.take_along_axis(tile, tile.shape[1] - 1 - lanes, axis=1)
    for bit in (4, 2, 1):
        up = pltpu.roll(tile, bit, 0)
        down = pltpu.roll(tile, tile.shape[0] - bit, 0)
        tile = jnp.where((rows & bit) != 0, up, down)
    return tile


def kernel(
    n_lon,
    forcing_hbm,
    coeffs_hbm,
    mask_hbm,
    fold_hbm,
    norm_hbm,
    out,
    forcing,
    coeffs,
    sea_mask,
    fold,
    norm,
    to_partner,
    to_mirror,
    north,
    south,
    ext,
    rim,
    weights,
    update,
    residual,
    iterate,
    load_sems,
    send_sems,
    recv_sems,
):
    levels, rows, cols = forcing.shape
    fields = 10 * levels
    pm_at = 8 * levels
    z_at = 9 * levels
    total = cols + 2 * DEPTH
    lon = lax.axis_index("lon")
    lat = lax.axis_index("lat")
    east = lax.rem(lon + 1, n_lon)
    west = lax.rem(lon + n_lon - 1, n_lon)
    mirror = n_lon - 1 - lon
    is_top = lat == 1

    loads = [
        pltpu.make_async_copy(source, target, load_sems.at[i])
        for i, (source, target) in enumerate(
            (
                (coeffs_hbm, coeffs),
                (forcing_hbm, forcing),
                (mask_hbm, sea_mask),
                (norm_hbm, norm),
                (fold_hbm, fold),
            )
        )
    ]
    for load in loads:
        load.start()

    barrier = pltpu.get_barrier_semaphore()

    def greet(where):
        pl.semaphore_signal(barrier, inc=1, device_id=where, device_id_type=MESH)

    greet({"lon": east})
    greet({"lon": west})
    greet({"lat": 1 - lat})

    @pl.when(is_top)
    def _():
        greet({"lon": mirror})

    for load in loads:
        load.wait()

    lane = lax.broadcasted_iota(jnp.int32, (1, cols), 1)
    offset = fold[pl.ds(lon, 1), :] - (n_lon * cols - 1 - (lon * cols + lane))
    offset = jnp.where(offset < 0, offset + n_lon * cols, offset)
    sub = lax.broadcasted_iota(jnp.int32, (8, cols), 0)
    at_fold = jnp.logical_and(sub == 7, is_top)

    def fields_of(k, start, stop):
        c = [coeffs[d, k, start:stop, :] for d in range(8)]
        diag_sum = c[0]
        for d in range(1, 8):
            diag_sum = diag_sum + c[d]
        sea = sea_mask[k, start:stop, :].astype(jnp.float32)
        pm = sea * (1.0 / (1.0 + diag_sum))
        if stop == rows:
            cut = rows - 8 - start
            north_edge = c[0][cut:]
            for d, (shift_lat, shift_lon) in enumerate(OFFSETS):
                if shift_lat == 1:
                    split = jnp.where(offset == 1 - shift_lon, north_edge, 0.0)
                    edge = jnp.where(at_fold, split, c[d][cut:])
                    c[d] = jnp.concatenate([c[d][:cut], edge], axis=0) if cut else edge
        z = sea * norm[k, start:stop, :] * forcing[k, start:stop, :]
        return [value * pm for value in c] + [pm, z]

    for k in range(levels):
        top = fields_of(k, rows - 8, rows)
        bottom = fields_of(k, 0, 8)
        for group in range(10):
            to_partner[group * levels + k] = jnp.where(is_top, bottom[group], top[group])
            turned = TURNED[group] if group < 8 else group
            to_mirror[turned * levels + k] = flipped(top[group])

    def remote(source, target, which, where):
        return pltpu.make_async_remote_copy(
            src_ref=source,
            dst_ref=target,
            send_sem=send_sems.at[which],
            recv_sem=recv_sems.at[which],
            device_id=where,
            device_id_type=MESH,
        )

    down = remote(to_partner, north, 0, {"lat": 1 - lat})
    across = remote(to_mirror, north, 1, {"lon": mirror})
    up = remote(to_partner, south, 2, {"lat": 1 - lat})

    @pl.when(is_top)
    def _():
        pl.semaphore_wait(barrier, 4)
        across.start()
        down.start()

    @pl.when(jnp.logical_not(is_top))
    def _():
        pl.semaphore_wait(barrier, 3)
        up.start()
        south[...] = jnp.zeros_like(south)

    padding = jnp.zeros((LANES - rows, cols), jnp.float32)
    for k in range(levels):
        for group, value in enumerate(fields_of(k, 0, rows)):
            whole = jnp.concatenate([value, padding], axis=0)
            ext[group * levels + k, DEPTH : DEPTH + cols, :] = whole.T

    ends = ((DEPTH, DEPTH + cols, west), (cols, 0, east))

    def strips(fields_ref, first):
        return [
            remote(
                fields_ref.at[:, pl.ds(source, DEPTH)],
                fields_ref.at[:, pl.ds(target, DEPTH)],
                first + i,
                {"lon": where},
            )
            for i, (source, target, where) in enumerate(ends)
        ]

    strip_sends = strips(ext, 3)
    rim_sends = strips(rim, 5)
    for send in strip_sends:
        send.start()

    @pl.when(is_top)
    def _():
        up.wait_recv()
        across.wait_recv()

    @pl.when(jnp.logical_not(is_top))
    def _():
        down.wait_recv()

    nothing = jnp.zeros((8, cols), jnp.float32)
    for first in range(0, fields, 4):
        halo = []
        for index in range(first, first + 4):
            plain = north[index]
            halo += [
                jnp.where(is_top, pltpu.roll(plain, 1, 1), plain),
                jnp.where(is_top, plain, 0.0),
                nothing,
                south[index],
            ]
        rim[first // 4, DEPTH : DEPTH + cols, :] = jnp.concatenate(halo, axis=0).T
    for send in rim_sends:
        send.start()
    for send in strip_sends:
        send.wait()

    def merge(start, stop):
        for index in range(fields):
            at = 32 * (index % 4)
            ext[index, start:stop, LANES - 32 :] = rim[index // 4, start:stop, at : at + 32]

    merge(DEPTH, DEPTH + cols)

    def place(start, stop):
        lanes = lax.broadcasted_iota(jnp.int32, (stop - start, LANES), 1)
        inside = jnp.logical_or(lanes < rows + 8, lanes >= LANES - 8)
        for k in range(levels):
            for d, (shift_lat, _) in enumerate(OFFSETS):
                value = jnp.where(inside, ext[d * levels + k, start:stop, :], 0.0)
                if shift_lat:
                    value = pltpu.roll(value, shift_lat % LANES, 1)
                weights[d * levels + k, start:stop, :] = value

    place(2 * DEPTH, DEPTH + cols)
    for send in rim_sends:
        send.wait()
    merge(0, DEPTH)
    merge(DEPTH + cols, total)

    lane_row = lax.broadcasted_iota(jnp.int32, (fields, LANES), 1)
    ghost = jnp.logical_and(jnp.logical_and(lane_row >= rows, lane_row < rows + 8), is_top)
    for seam in (DEPTH, DEPTH + cols):
        before = pltpu.roll(ext[:, seam - 1, :], LANES - 8, 1)
        ext[:, seam, :] = jnp.where(ghost, before, ext[:, seam, :])
    place(0, 2 * DEPTH)
    place(DEPTH + cols, total)

    chunks = total // 8
    sub_all = lax.broadcasted_iota(jnp.int32, (8, LANES), 0)
    low, high = sub_all == 0, sub_all == 7

    def parts(k, s):
        at = pl.ds(8 * s, 8)
        u = update[k, at, :]
        by_lat = {0: u, 1: pltpu.roll(u, 1, 1), -1: pltpu.roll(u, LANES - 1, 1)}
        sums = {}
        for d, (shift_lat, shift_lon) in enumerate(OFFSETS):
            term = weights[d * levels + k, at, :] * by_lat[shift_lat]
            sums[shift_lon] = sums[shift_lon] + term if shift_lon in sums else term
        return sums[-1], sums[0], sums[1], u

    def sweep(keep_ratio, gain):
        held = [[None] * chunks for _ in range(levels)]
        for s in range(chunks + 1):
            for k in range(levels):
                if s < chunks:
                    held[k][s] = parts(k, s)
                if s == 0:
                    continue
                t = s - 1
                here = held[k][t]
                left = held[k][t - 1][2] if t else here[2]
                right = held[k][s][0] if s < chunks else here[0]
                gained = (
                    here[1]
                    + pltpu.roll(jnp.where(high, left, here[2]), 1, 0)
                    + pltpu.roll(jnp.where(low, right, here[0]), 7, 0)
                )
                at = pl.ds(8 * t, 8)
                res = (residual[k, at, :] - here[3]) + gained
                new = keep_ratio * here[3] + gain * res
                residual[k, at, :] = res
                update[k, at, :] = new
                iterate[k, at, :] = iterate[k, at, :] + new

    sigma_ratio = CENTRE_VALUE / HALF_WIDTH
    ratio_now = 1.0 / sigma_ratio
    factors = []
    for _ in range(ITERS):
        ratio_next = 1.0 / (2.0 * sigma_ratio - ratio_now)
        factors.append((ratio_next * ratio_now, 2.0 * ratio_next / HALF_WIDTH))
        ratio_now = ratio_next

    def pick(values, i):
        chosen = jnp.float32(values[-1])
        for n in range(len(values) - 1):
            chosen = jnp.where(i == n, jnp.float32(values[n]), chosen)
        return chosen

    for step in range(STEPS):
        for k in range(levels):
            start = ext[z_at + k] if step == 0 else ext[pm_at + k] * iterate[k]
            residual[k] = start
            first = start * (1.0 / CENTRE_VALUE)
            update[k] = first
            iterate[k] = first

        @pl.loop(0, ITERS)
        def _(i):
            sweep(pick([f[0] for f in factors], i), pick([f[1] for f in factors], i))

    for k in range(levels):
        own = (ext[pm_at + k, DEPTH : DEPTH + cols] * iterate[k, DEPTH : DEPTH + cols]).T
        out[k] = norm[k] * own[:rows]

    @pl.when(is_top)
    def _():
        down.wait_send()
        across.wait_send()

    @pl.when(jnp.logical_not(is_top))
    def _():
        up.wait_send()


def body(n_lon, forcing, coeffs, sea_mask, fold_pair, norm_scale):
    levels, rows, cols = forcing.shape
    fields = 10 * levels
    total = cols + 2 * DEPTH
    edge = pltpu.VMEM((fields, 8, cols), jnp.float32)
    tile = pltpu.VMEM(forcing.shape, jnp.float32)
    field = pltpu.VMEM((levels, total, LANES), jnp.float32)
    return pl.pallas_call(
        functools.partial(kernel, n_lon),
        out_shape=jax.ShapeDtypeStruct(forcing.shape, jnp.float32),
        in_specs=[pl.BlockSpec(memory_space=pltpu.HBM)] * 5,
        out_specs=pl.BlockSpec(memory_space=pltpu.VMEM),
        scratch_shapes=[
            tile,
            pltpu.VMEM(coeffs.shape, jnp.float32),
            pltpu.VMEM(sea_mask.shape, jnp.int32),
            pltpu.VMEM((n_lon, cols), jnp.int32),
            tile,
            edge,
            edge,
            edge,
            edge,
            pltpu.VMEM((fields, total, LANES), jnp.float32),
            pltpu.VMEM((fields // 4, total, LANES), jnp.float32),
            pltpu.VMEM((8 * levels, total, LANES), jnp.float32),
            field,
            field,
            field,
            pltpu.SemaphoreType.DMA((5,)),
            pltpu.SemaphoreType.DMA((7,)),
            pltpu.SemaphoreType.DMA((7,)),
        ],
        compiler_params=pltpu.CompilerParams(
            collective_id=0, has_side_effects=True, vmem_limit_bytes=60 * 1024 * 1024
        ),
    )(forcing, coeffs, sea_mask, fold_pair.reshape(n_lon, cols), norm_scale)


def solution(mesh):
    placed = (
        P("member", "lat", "lon"),
        P(None, None, "lat", "lon"),
        P(None, "lat", "lon"),
        P(),
        P(None, "lat", "lon"),
    )
    return jax.shard_map(
        functools.partial(body, mesh.shape["lon"]),
        mesh=mesh,
        in_specs=placed,
        out_specs=P("member", "lat", "lon"),
        check_vma=False,
    )
```

```python
import functools

import jax
import jax.numpy as jnp
from jax import lax
from jax.experimental import pallas as pl
from jax.experimental.pallas import tpu as pltpu
from jax.sharding import PartitionSpec as P

STEPS = 2
ITERS = 4
DEPTH = STEPS * ITERS
LANES = 128

OFFSETS = ((1, 0), (-1, 0), (0, 1), (0, -1), (1, 1), (1, -1), (-1, 1), (-1, -1))
TURNED = tuple(OFFSETS.index((-r, -c)) for r, c in OFFSETS)
CENTRE_VALUE = 1.05
HALF_WIDTH = 0.9
MESH = pl.DeviceIdType.MESH


def flipped(tile):
    lanes = lax.broadcasted_iota(jnp.int32, tile.shape, 1)
    rows = lax.broadcasted_iota(jnp.int32, tile.shape, 0)
    tile = jnp.take_along_axis(tile, tile.shape[1] - 1 - lanes, axis=1)
    for bit in (4, 2, 1):
        up = pltpu.roll(tile, bit, 0)
        down = pltpu.roll(tile, tile.shape[0] - bit, 0)
        tile = jnp.where((rows & bit) != 0, up, down)
    return tile


def kernel(
    n_lon,
    forcing_hbm,
    coeffs_hbm,
    mask_hbm,
    fold_hbm,
    norm_hbm,
    out,
    forcing,
    coeffs,
    sea_mask,
    fold,
    norm,
    to_partner,
    to_mirror,
    north,
    south,
    ext,
    rim,
    weights,
    update,
    residual,
    iterate,
    load_sems,
    send_sems,
    recv_sems,
):
    levels, rows, cols = forcing.shape
    fields = 10 * levels
    pm_at = 8 * levels
    z_at = 9 * levels
    total = cols + 2 * DEPTH
    lon = lax.axis_index("lon")
    lat = lax.axis_index("lat")
    east = lax.rem(lon + 1, n_lon)
    west = lax.rem(lon + n_lon - 1, n_lon)
    mirror = n_lon - 1 - lon
    is_top = lat == 1

    loads = [
        pltpu.make_async_copy(source, target, load_sems.at[i])
        for i, (source, target) in enumerate(
            (
                (coeffs_hbm, coeffs),
                (forcing_hbm, forcing),
                (mask_hbm, sea_mask),
                (norm_hbm, norm),
                (fold_hbm, fold),
            )
        )
    ]
    for load in loads:
        load.start()

    barrier = pltpu.get_barrier_semaphore()

    def greet(where):
        pl.semaphore_signal(barrier, inc=1, device_id=where, device_id_type=MESH)

    greet({"lon": east})
    greet({"lon": west})
    greet({"lat": 1 - lat})

    @pl.when(is_top)
    def _():
        greet({"lon": mirror})

    for load in loads:
        load.wait()

    lane = lax.broadcasted_iota(jnp.int32, (1, cols), 1)
    offset = fold[pl.ds(lon, 1), :] - (n_lon * cols - 1 - (lon * cols + lane))
    offset = jnp.where(offset < 0, offset + n_lon * cols, offset)
    sub = lax.broadcasted_iota(jnp.int32, (8, cols), 0)
    at_fold = jnp.logical_and(sub == 7, is_top)

    def fields_of(k, start, stop):
        c = [coeffs[d, k, start:stop, :] for d in range(8)]
        diag_sum = c[0]
        for d in range(1, 8):
            diag_sum = diag_sum + c[d]
        sea = sea_mask[k, start:stop, :].astype(jnp.float32)
        pm = sea * (1.0 / (1.0 + diag_sum))
        if stop == rows:
            cut = rows - 8 - start
            north_edge = c[0][cut:]
            for d, (shift_lat, shift_lon) in enumerate(OFFSETS):
                if shift_lat == 1:
                    split = jnp.where(offset == 1 - shift_lon, north_edge, 0.0)
                    edge = jnp.where(at_fold, split, c[d][cut:])
                    c[d] = jnp.concatenate([c[d][:cut], edge], axis=0) if cut else edge
        z = sea * norm[k, start:stop, :] * forcing[k, start:stop, :]
        return [value * pm for value in c] + [pm, z]

    for k in range(levels):
        top = fields_of(k, rows - 8, rows)
        bottom = fields_of(k, 0, 8)
        for group in range(10):
            to_partner[group * levels + k] = jnp.where(is_top, bottom[group], top[group])
            turned = TURNED[group] if group < 8 else group
            to_mirror[turned * levels + k] = flipped(top[group])

    def remote(source, target, which, where):
        return pltpu.make_async_remote_copy(
            src_ref=source,
            dst_ref=target,
            send_sem=send_sems.at[which],
            recv_sem=recv_sems.at[which],
            device_id=where,
            device_id_type=MESH,
        )

    down = remote(to_partner, north, 0, {"lat": 1 - lat})
    across = remote(to_mirror, north, 1, {"lon": mirror})
    up = remote(to_partner, south, 2, {"lat": 1 - lat})

    padding = jnp.zeros((LANES - rows, cols), jnp.float32)
    for k in range(levels):
        for group, value in enumerate(fields_of(k, 0, rows)):
            whole = jnp.concatenate([value, padding], axis=0)
            ext[group * levels + k, DEPTH : DEPTH + cols, :] = whole.T

    ends = ((DEPTH, DEPTH + cols, west), (cols, 0, east))

    def strips(fields_ref, count, first):
        return [
            remote(
                fields_ref.at[pl.ds(0, count), pl.ds(source, DEPTH)],
                fields_ref.at[pl.ds(0, count), pl.ds(target, DEPTH)],
                first + i,
                {"lon": where},
            )
            for i, (source, target, where) in enumerate(ends)
        ]

    sent = fields * 3 // 4

    def thirds():
        for i in range(sent):
            yield i, sent + i // 3, 32 * (i % 3)

    for start in (DEPTH, cols):
        for carrier, rider, at in thirds():
            piece = ext[rider, start : start + DEPTH, at : at + 32]
            ext[carrier, start : start + DEPTH, LANES - 32 :] = piece

    @pl.when(is_top)
    def _():
        pl.semaphore_wait(barrier, 4)
        across.start()
        down.start()

    @pl.when(jnp.logical_not(is_top))
    def _():
        pl.semaphore_wait(barrier, 3)
        up.start()
        south[...] = jnp.zeros_like(south)

    strip_sends = strips(ext, sent, 3)
    rim_sends = strips(rim, fields // 4, 5)
    for send in strip_sends:
        send.start()

    @pl.when(is_top)
    def _():
        up.wait_recv()
        across.wait_recv()

    @pl.when(jnp.logical_not(is_top))
    def _():
        down.wait_recv()

    nothing = jnp.zeros((8, cols), jnp.float32)
    for first in range(0, fields, 4):
        halo = []
        for index in range(first, first + 4):
            plain = north[index]
            halo += [
                jnp.where(is_top, pltpu.roll(plain, 1, 1), plain),
                jnp.where(is_top, plain, 0.0),
                nothing,
                south[index],
            ]
        rim[first // 4, DEPTH : DEPTH + cols, :] = jnp.concatenate(halo, axis=0).T
    for send in rim_sends:
        send.start()
    for send in strip_sends:
        send.wait()

    def merge(start, stop):
        for index in range(fields):
            at = 32 * (index % 4)
            ext[index, start:stop, LANES - 32 :] = rim[index // 4, start:stop, at : at + 32]

    for start in (0, DEPTH + cols):
        for carrier, rider, at in thirds():
            piece = ext[carrier, start : start + DEPTH, LANES - 32 :]
            ext[rider, start : start + DEPTH, at : at + 32] = piece
    merge(DEPTH, DEPTH + cols)

    def place(start, stop):
        lanes = lax.broadcasted_iota(jnp.int32, (stop - start, LANES), 1)
        inside = jnp.logical_or(lanes < rows + 8, lanes >= LANES - 8)
        for k in range(levels):
            for d, (shift_lat, _) in enumerate(OFFSETS):
                value = jnp.where(inside, ext[d * levels + k, start:stop, :], 0.0)
                if shift_lat:
                    value = pltpu.roll(value, shift_lat % LANES, 1)
                weights[d * levels + k, start:stop, :] = value

    place(2 * DEPTH, DEPTH + cols)
    for send in rim_sends:
        send.wait()
    merge(0, DEPTH)
    merge(DEPTH + cols, total)

    lane_row = lax.broadcasted_iota(jnp.int32, (fields, LANES), 1)
    ghost = jnp.logical_and(jnp.logical_and(lane_row >= rows, lane_row < rows + 8), is_top)
    for seam in (DEPTH, DEPTH + cols):
        before = pltpu.roll(ext[:, seam - 1, :], LANES - 8, 1)
        ext[:, seam, :] = jnp.where(ghost, before, ext[:, seam, :])
    place(0, 2 * DEPTH)
    place(DEPTH + cols, total)

    chunks = total // 8
    sub_all = lax.broadcasted_iota(jnp.int32, (8, LANES), 0)
    low, high = sub_all == 0, sub_all == 7

    def parts(k, s):
        at = pl.ds(8 * s, 8)
        u = update[k, at, :]
        by_lat = {0: u, 1: pltpu.roll(u, 1, 1), -1: pltpu.roll(u, LANES - 1, 1)}
        sums = {}
        for d, (shift_lat, shift_lon) in enumerate(OFFSETS):
            term = weights[d * levels + k, at, :] * by_lat[shift_lat]
            sums[shift_lon] = sums[shift_lon] + term if shift_lon in sums else term
        return sums[-1], sums[0], sums[1], u

    def sweep(keep_ratio, gain):
        held = [[None] * chunks for _ in range(levels)]
        for s in range(chunks + 1):
            for k in range(levels):
                if s < chunks:
                    held[k][s] = parts(k, s)
                if s == 0:
                    continue
                t = s - 1
                here = held[k][t]
                left = held[k][t - 1][2] if t else here[2]
                right = held[k][s][0] if s < chunks else here[0]
                gained = (
                    here[1]
                    + pltpu.roll(jnp.where(high, left, here[2]), 1, 0)
                    + pltpu.roll(jnp.where(low, right, here[0]), 7, 0)
                )
                at = pl.ds(8 * t, 8)
                res = (residual[k, at, :] - here[3]) + gained
                new = keep_ratio * here[3] + gain * res
                residual[k, at, :] = res
                update[k, at, :] = new
                iterate[k, at, :] = iterate[k, at, :] + new

    sigma_ratio = CENTRE_VALUE / HALF_WIDTH
    ratio_now = 1.0 / sigma_ratio
    factors = []
    for _ in range(ITERS):
        ratio_next = 1.0 / (2.0 * sigma_ratio - ratio_now)
        factors.append((ratio_next * ratio_now, 2.0 * ratio_next / HALF_WIDTH))
        ratio_now = ratio_next

    def pick(values, i):
        chosen = jnp.float32(values[-1])
        for n in range(len(values) - 1):
            chosen = jnp.where(i == n, jnp.float32(values[n]), chosen)
        return chosen

    for step in range(STEPS):
        for k in range(levels):
            start = ext[z_at + k] if step == 0 else ext[pm_at + k] * iterate[k]
            residual[k] = start
            first = start * (1.0 / CENTRE_VALUE)
            update[k] = first
            iterate[k] = first

        @pl.loop(0, ITERS)
        def _(i):
            sweep(pick([f[0] for f in factors], i), pick([f[1] for f in factors], i))

    for k in range(levels):
        own = (ext[pm_at + k, DEPTH : DEPTH + cols] * iterate[k, DEPTH : DEPTH + cols]).T
        out[k] = norm[k] * own[:rows]

    @pl.when(is_top)
    def _():
        down.wait_send()
        across.wait_send()

    @pl.when(jnp.logical_not(is_top))
    def _():
        up.wait_send()


def body(n_lon, forcing, coeffs, sea_mask, fold_pair, norm_scale):
    levels, rows, cols = forcing.shape
    fields = 10 * levels
    total = cols + 2 * DEPTH
    edge = pltpu.VMEM((fields, 8, cols), jnp.float32)
    tile = pltpu.VMEM(forcing.shape, jnp.float32)
    field = pltpu.VMEM((levels, total, LANES), jnp.float32)
    return pl.pallas_call(
        functools.partial(kernel, n_lon),
        out_shape=jax.ShapeDtypeStruct(forcing.shape, jnp.float32),
        in_specs=[pl.BlockSpec(memory_space=pltpu.HBM)] * 5,
        out_specs=pl.BlockSpec(memory_space=pltpu.VMEM),
        scratch_shapes=[
            tile,
            pltpu.VMEM(coeffs.shape, jnp.float32),
            pltpu.VMEM(sea_mask.shape, jnp.int32),
            pltpu.VMEM((n_lon, cols), jnp.int32),
            tile,
            edge,
            edge,
            edge,
            edge,
            pltpu.VMEM((fields, total, LANES), jnp.float32),
            pltpu.VMEM((fields // 4, total, LANES), jnp.float32),
            pltpu.VMEM((8 * levels, total, LANES), jnp.float32),
            field,
            field,
            field,
            pltpu.SemaphoreType.DMA((5,)),
            pltpu.SemaphoreType.DMA((7,)),
            pltpu.SemaphoreType.DMA((7,)),
        ],
        compiler_params=pltpu.CompilerParams(
            collective_id=0, has_side_effects=True, vmem_limit_bytes=60 * 1024 * 1024
        ),
    )(forcing, coeffs, sea_mask, fold_pair.reshape(n_lon, cols), norm_scale)


def solution(mesh):
    placed = (
        P("member", "lat", "lon"),
        P(None, None, "lat", "lon"),
        P(None, "lat", "lon"),
        P(),
        P(None, "lat", "lon"),
    )
    return jax.shard_map(
        functools.partial(body, mesh.shape["lon"]),
        mesh=mesh,
        in_specs=placed,
        out_specs=P("member", "lat", "lon"),
        check_vma=False,
    )
```

```python
import functools

import jax
import jax.numpy as jnp
from jax import lax
from jax.experimental import pallas as pl
from jax.experimental.pallas import tpu as pltpu
from jax.sharding import PartitionSpec as P

STEPS = 2
ITERS = 4
DEPTH = STEPS * ITERS
LANES = 128

OFFSETS = ((1, 0), (-1, 0), (0, 1), (0, -1), (1, 1), (1, -1), (-1, 1), (-1, -1))
TURNED = tuple(OFFSETS.index((-r, -c)) for r, c in OFFSETS)
CENTRE_VALUE = 1.05
HALF_WIDTH = 0.9
MESH = pl.DeviceIdType.MESH


def flipped(tile):
    lanes = lax.broadcasted_iota(jnp.int32, tile.shape, 1)
    rows = lax.broadcasted_iota(jnp.int32, tile.shape, 0)
    tile = jnp.take_along_axis(tile, tile.shape[1] - 1 - lanes, axis=1)
    for bit in (4, 2, 1):
        up = pltpu.roll(tile, bit, 0)
        down = pltpu.roll(tile, tile.shape[0] - bit, 0)
        tile = jnp.where((rows & bit) != 0, up, down)
    return tile


def kernel(
    n_lon,
    forcing_hbm,
    coeffs_hbm,
    mask_hbm,
    fold_hbm,
    norm_hbm,
    out,
    forcing,
    coeffs,
    sea_mask,
    fold,
    norm,
    to_partner,
    to_mirror,
    north,
    south,
    ext,
    rim,
    weights,
    update,
    residual,
    iterate,
    load_sems,
    send_sems,
    recv_sems,
):
    levels, rows, cols = forcing.shape
    fields = 10 * levels
    pm_at = 8 * levels
    z_at = 9 * levels
    total = cols + 2 * DEPTH
    lon = lax.axis_index("lon")
    lat = lax.axis_index("lat")
    east = lax.rem(lon + 1, n_lon)
    west = lax.rem(lon + n_lon - 1, n_lon)
    mirror = n_lon - 1 - lon
    is_top = lat == 1

    loads = [
        pltpu.make_async_copy(source, target, load_sems.at[i])
        for i, (source, target) in enumerate(
            (
                (coeffs_hbm, coeffs),
                (forcing_hbm, forcing),
                (mask_hbm, sea_mask),
                (norm_hbm, norm),
                (fold_hbm, fold),
            )
        )
    ]
    for load in loads:
        load.start()

    barrier = pltpu.get_barrier_semaphore()

    def greet(where):
        pl.semaphore_signal(barrier, inc=1, device_id=where, device_id_type=MESH)

    greet({"lon": east})
    greet({"lon": west})
    greet({"lat": 1 - lat})

    @pl.when(is_top)
    def _():
        greet({"lon": mirror})

    for load in loads:
        load.wait()

    lane = lax.broadcasted_iota(jnp.int32, (1, cols), 1)
    offset = fold[pl.ds(lon, 1), :] - (n_lon * cols - 1 - (lon * cols + lane))
    offset = jnp.where(offset < 0, offset + n_lon * cols, offset)
    sub = lax.broadcasted_iota(jnp.int32, (8, cols), 0)
    at_fold = jnp.logical_and(sub == 7, is_top)

    def fields_of(k, start, stop):
        c = [coeffs[d, k, start:stop, :] for d in range(8)]
        diag_sum = c[0]
        for d in range(1, 8):
            diag_sum = diag_sum + c[d]
        sea = sea_mask[k, start:stop, :].astype(jnp.float32)
        pm = sea * (1.0 / (1.0 + diag_sum))
        if stop == rows:
            cut = rows - 8 - start
            north_edge = c[0][cut:]
            for d, (shift_lat, shift_lon) in enumerate(OFFSETS):
                if shift_lat == 1:
                    split = jnp.where(offset == 1 - shift_lon, north_edge, 0.0)
                    edge = jnp.where(at_fold, split, c[d][cut:])
                    c[d] = jnp.concatenate([c[d][:cut], edge], axis=0) if cut else edge
        z = sea * norm[k, start:stop, :] * forcing[k, start:stop, :]
        return [value * pm for value in c] + [pm, z]

    for k in range(levels):
        top = fields_of(k, rows - 8, rows)
        bottom = fields_of(k, 0, 8)
        for group in range(10):
            to_partner[group * levels + k] = jnp.where(is_top, bottom[group], top[group])
            turned = TURNED[group] if group < 8 else group
            to_mirror[turned * levels + k] = flipped(top[group])

    def remote(source, target, which, where):
        return pltpu.make_async_remote_copy(
            src_ref=source,
            dst_ref=target,
            send_sem=send_sems.at[which],
            recv_sem=recv_sems.at[which],
            device_id=where,
            device_id_type=MESH,
        )

    middle = 4 * ((fields // 4 + 1) // 2)
    halves = ((0, middle), (middle, fields))

    def in_halves(source, target, which, where):
        return [
            remote(
                source.at[pl.ds(a, b - a)], target.at[pl.ds(a, b - a)], which + i, where
            )
            for i, (a, b) in enumerate(halves)
        ]

    down = in_halves(to_partner, north, 0, {"lat": 1 - lat})
    across = in_halves(to_mirror, north, 2, {"lon": mirror})
    up = in_halves(to_partner, south, 4, {"lat": 1 - lat})

    padding = jnp.zeros((LANES - rows, cols), jnp.float32)
    for k in range(levels):
        for group, value in enumerate(fields_of(k, 0, rows)):
            whole = jnp.concatenate([value, padding], axis=0)
            ext[group * levels + k, DEPTH : DEPTH + cols, :] = whole.T

    ends = ((DEPTH, DEPTH + cols, west), (cols, 0, east))

    def strips(fields_ref, begin, count, first):
        return [
            remote(
                fields_ref.at[pl.ds(begin, count), pl.ds(source, DEPTH)],
                fields_ref.at[pl.ds(begin, count), pl.ds(target, DEPTH)],
                first + i,
                {"lon": where},
            )
            for i, (source, target, where) in enumerate(ends)
        ]

    sent = fields * 3 // 4

    def thirds():
        for i in range(sent):
            yield i, sent + i // 3, 32 * (i % 3)

    for start in (DEPTH, cols):
        for carrier, rider, at in thirds():
            piece = ext[rider, start : start + DEPTH, at : at + 32]
            ext[carrier, start : start + DEPTH, LANES - 32 :] = piece

    @pl.when(is_top)
    def _():
        pl.semaphore_wait(barrier, 4)
        for i in range(2):
            across[i].start()
            down[i].start()

    @pl.when(jnp.logical_not(is_top))
    def _():
        pl.semaphore_wait(barrier, 3)
        for i in range(2):
            up[i].start()
        south[...] = jnp.zeros_like(south)

    strip_sends = strips(ext, 0, sent, 6)
    rim_sends = [
        strips(rim, a // 4, (b - a) // 4, 8 + 2 * i) for i, (a, b) in enumerate(halves)
    ]
    for send in strip_sends:
        send.start()

    nothing = jnp.zeros((8, cols), jnp.float32)
    for half in range(2):

        @pl.when(is_top)
        def _():
            up[half].wait_recv()
            across[half].wait_recv()

        @pl.when(jnp.logical_not(is_top))
        def _():
            down[half].wait_recv()

        for first in range(*halves[half], 4):
            halo = []
            for index in range(first, first + 4):
                plain = north[index]
                halo += [
                    jnp.where(is_top, pltpu.roll(plain, 1, 1), plain),
                    jnp.where(is_top, plain, 0.0),
                    nothing,
                    south[index],
                ]
            rim[first // 4, DEPTH : DEPTH + cols, :] = jnp.concatenate(halo, axis=0).T
        for send in rim_sends[half]:
            send.start()
    for send in strip_sends:
        send.wait()

    def merge(start, stop):
        for index in range(fields):
            at = 32 * (index % 4)
            ext[index, start:stop, LANES - 32 :] = rim[index // 4, start:stop, at : at + 32]

    for start in (0, DEPTH + cols):
        for carrier, rider, at in thirds():
            piece = ext[carrier, start : start + DEPTH, LANES - 32 :]
            ext[rider, start : start + DEPTH, at : at + 32] = piece
    merge(DEPTH, DEPTH + cols)

    def place(start, stop):
        lanes = lax.broadcasted_iota(jnp.int32, (stop - start, LANES), 1)
        inside = jnp.logical_or(lanes < rows + 8, lanes >= LANES - 8)
        for k in range(levels):
            for d, (shift_lat, _) in enumerate(OFFSETS):
                value = jnp.where(inside, ext[d * levels + k, start:stop, :], 0.0)
                if shift_lat:
                    value = pltpu.roll(value, shift_lat % LANES, 1)
                weights[d * levels + k, start:stop, :] = value

    place(2 * DEPTH, DEPTH + cols)
    for send in rim_sends[0] + rim_sends[1]:
        send.wait()
    merge(0, DEPTH)
    merge(DEPTH + cols, total)

    lane_row = lax.broadcasted_iota(jnp.int32, (fields, LANES), 1)
    ghost = jnp.logical_and(jnp.logical_and(lane_row >= rows, lane_row < rows + 8), is_top)
    for seam in (DEPTH, DEPTH + cols):
        before = pltpu.roll(ext[:, seam - 1, :], LANES - 8, 1)
        ext[:, seam, :] = jnp.where(ghost, before, ext[:, seam, :])
    place(0, 2 * DEPTH)
    place(DEPTH + cols, total)

    chunks = total // 8
    sub_all = lax.broadcasted_iota(jnp.int32, (8, LANES), 0)
    low, high = sub_all == 0, sub_all == 7

    def parts(k, s):
        at = pl.ds(8 * s, 8)
        u = update[k, at, :]
        by_lat = {0: u, 1: pltpu.roll(u, 1, 1), -1: pltpu.roll(u, LANES - 1, 1)}
        sums = {}
        for d, (shift_lat, shift_lon) in enumerate(OFFSETS):
            term = weights[d * levels + k, at, :] * by_lat[shift_lat]
            sums[shift_lon] = sums[shift_lon] + term if shift_lon in sums else term
        return sums[-1], sums[0], sums[1], u

    def sweep(keep_ratio, gain):
        held = [[None] * chunks for _ in range(levels)]
        for s in range(chunks + 1):
            for k in range(levels):
                if s < chunks:
                    held[k][s] = parts(k, s)
                if s == 0:
                    continue
                t = s - 1
                here = held[k][t]
                left = held[k][t - 1][2] if t else here[2]
                right = held[k][s][0] if s < chunks else here[0]
                gained = (
                    here[1]
                    + pltpu.roll(jnp.where(high, left, here[2]), 1, 0)
                    + pltpu.roll(jnp.where(low, right, here[0]), 7, 0)
                )
                at = pl.ds(8 * t, 8)
                res = (residual[k, at, :] - here[3]) + gained
                new = keep_ratio * here[3] + gain * res
                residual[k, at, :] = res
                update[k, at, :] = new
                iterate[k, at, :] = iterate[k, at, :] + new

    sigma_ratio = CENTRE_VALUE / HALF_WIDTH
    ratio_now = 1.0 / sigma_ratio
    factors = []
    for _ in range(ITERS):
        ratio_next = 1.0 / (2.0 * sigma_ratio - ratio_now)
        factors.append((ratio_next * ratio_now, 2.0 * ratio_next / HALF_WIDTH))
        ratio_now = ratio_next

    def pick(values, i):
        chosen = jnp.float32(values[-1])
        for n in range(len(values) - 1):
            chosen = jnp.where(i == n, jnp.float32(values[n]), chosen)
        return chosen

    for step in range(STEPS):
        for k in range(levels):
            start = ext[z_at + k] if step == 0 else ext[pm_at + k] * iterate[k]
            residual[k] = start
            first = start * (1.0 / CENTRE_VALUE)
            update[k] = first
            iterate[k] = first

        @pl.loop(0, ITERS)
        def _(i):
            sweep(pick([f[0] for f in factors], i), pick([f[1] for f in factors], i))

    for k in range(levels):
        own = (ext[pm_at + k, DEPTH : DEPTH + cols] * iterate[k, DEPTH : DEPTH + cols]).T
        out[k] = norm[k] * own[:rows]

    @pl.when(is_top)
    def _():
        for i in range(2):
            down[i].wait_send()
            across[i].wait_send()

    @pl.when(jnp.logical_not(is_top))
    def _():
        for i in range(2):
            up[i].wait_send()


def body(n_lon, forcing, coeffs, sea_mask, fold_pair, norm_scale):
    levels, rows, cols = forcing.shape
    fields = 10 * levels
    total = cols + 2 * DEPTH
    edge = pltpu.VMEM((fields, 8, cols), jnp.float32)
    tile = pltpu.VMEM(forcing.shape, jnp.float32)
    field = pltpu.VMEM((levels, total, LANES), jnp.float32)
    return pl.pallas_call(
        functools.partial(kernel, n_lon),
        out_shape=jax.ShapeDtypeStruct(forcing.shape, jnp.float32),
        in_specs=[pl.BlockSpec(memory_space=pltpu.HBM)] * 5,
        out_specs=pl.BlockSpec(memory_space=pltpu.VMEM),
        scratch_shapes=[
            tile,
            pltpu.VMEM(coeffs.shape, jnp.float32),
            pltpu.VMEM(sea_mask.shape, jnp.int32),
            pltpu.VMEM((n_lon, cols), jnp.int32),
            tile,
            edge,
            edge,
            edge,
            edge,
            pltpu.VMEM((fields, total, LANES), jnp.float32),
            pltpu.VMEM((fields // 4, total, LANES), jnp.float32),
            pltpu.VMEM((8 * levels, total, LANES), jnp.float32),
            field,
            field,
            field,
            pltpu.SemaphoreType.DMA((5,)),
            pltpu.SemaphoreType.DMA((12,)),
            pltpu.SemaphoreType.DMA((12,)),
        ],
        compiler_params=pltpu.CompilerParams(
            collective_id=0, has_side_effects=True, vmem_limit_bytes=60 * 1024 * 1024
        ),
    )(forcing, coeffs, sea_mask, fold_pair.reshape(n_lon, cols), norm_scale)


def solution(mesh):
    placed = (
        P("member", "lat", "lon"),
        P(None, None, "lat", "lon"),
        P(None, "lat", "lon"),
        P(),
        P(None, "lat", "lon"),
    )
    return jax.shard_map(
        functools.partial(body, mesh.shape["lon"]),
        mesh=mesh,
        in_specs=placed,
        out_specs=P("member", "lat", "lon"),
        check_vma=False,
    )
```

```python
import functools

import jax
import jax.numpy as jnp
from jax import lax
from jax.experimental import pallas as pl
from jax.experimental.pallas import tpu as pltpu
from jax.sharding import PartitionSpec as P

STEPS = 2
ITERS = 4
DEPTH = STEPS * ITERS
LANES = 128

OFFSETS = ((1, 0), (-1, 0), (0, 1), (0, -1), (1, 1), (1, -1), (-1, 1), (-1, -1))
TURNED = tuple(OFFSETS.index((-r, -c)) for r, c in OFFSETS)
CENTRE_VALUE = 1.05
HALF_WIDTH = 0.9
MESH = pl.DeviceIdType.MESH


def flipped(tile):
    lanes = lax.broadcasted_iota(jnp.int32, tile.shape, 1)
    rows = lax.broadcasted_iota(jnp.int32, tile.shape, 0)
    tile = jnp.take_along_axis(tile, tile.shape[1] - 1 - lanes, axis=1)
    for bit in (4, 2, 1):
        up = pltpu.roll(tile, bit, 0)
        down = pltpu.roll(tile, tile.shape[0] - bit, 0)
        tile = jnp.where((rows & bit) != 0, up, down)
    return tile


def kernel(
    n_lon,
    forcing_hbm,
    coeffs_hbm,
    mask_hbm,
    fold_hbm,
    norm_hbm,
    out,
    forcing,
    coeffs,
    sea_mask,
    fold,
    norm,
    to_partner,
    to_mirror,
    north,
    south,
    ext,
    rim,
    weights,
    update,
    residual,
    iterate,
    load_sems,
    send_sems,
    recv_sems,
):
    levels, rows, cols = forcing.shape
    fields = 10 * levels
    pm_at = 8 * levels
    z_at = 9 * levels
    total = cols + 2 * DEPTH
    lon = lax.axis_index("lon")
    lat = lax.axis_index("lat")
    east = lax.rem(lon + 1, n_lon)
    west = lax.rem(lon + n_lon - 1, n_lon)
    mirror = n_lon - 1 - lon
    is_top = lat == 1

    loads = [
        pltpu.make_async_copy(source, target, load_sems.at[i])
        for i, (source, target) in enumerate(
            (
                (coeffs_hbm, coeffs),
                (forcing_hbm, forcing),
                (mask_hbm, sea_mask),
                (norm_hbm, norm),
                (fold_hbm, fold),
            )
        )
    ]
    for load in loads:
        load.start()

    barrier = pltpu.get_barrier_semaphore()

    def greet(where):
        pl.semaphore_signal(barrier, inc=1, device_id=where, device_id_type=MESH)

    greet({"lon": east})
    greet({"lon": west})
    greet({"lat": 1 - lat})

    @pl.when(is_top)
    def _():
        greet({"lon": mirror})

    for load in loads:
        load.wait()

    lane = lax.broadcasted_iota(jnp.int32, (1, cols), 1)
    offset = fold[pl.ds(lon, 1), :] - (n_lon * cols - 1 - (lon * cols + lane))
    offset = jnp.where(offset < 0, offset + n_lon * cols, offset)
    sub = lax.broadcasted_iota(jnp.int32, (8, cols), 0)
    at_fold = jnp.logical_and(sub == 7, is_top)

    def fields_of(k, start, stop):
        c = [coeffs[d, k, start:stop, :] for d in range(8)]
        diag_sum = c[0]
        for d in range(1, 8):
            diag_sum = diag_sum + c[d]
        sea = sea_mask[k, start:stop, :].astype(jnp.float32)
        pm = sea * (1.0 / (1.0 + diag_sum))
        if stop == rows:
            cut = rows - 8 - start
            north_edge = c[0][cut:]
            for d, (shift_lat, shift_lon) in enumerate(OFFSETS):
                if shift_lat == 1:
                    split = jnp.where(offset == 1 - shift_lon, north_edge, 0.0)
                    edge = jnp.where(at_fold, split, c[d][cut:])
                    c[d] = jnp.concatenate([c[d][:cut], edge], axis=0) if cut else edge
        z = sea * norm[k, start:stop, :] * forcing[k, start:stop, :]
        return [value * pm for value in c] + [pm, z]

    for k in range(levels):
        top = fields_of(k, rows - 8, rows)
        bottom = fields_of(k, 0, 8)
        for group in range(10):
            to_partner[group * levels + k] = jnp.where(is_top, bottom[group], top[group])
            turned = TURNED[group] if group < 8 else group
            to_mirror[turned * levels + k] = flipped(top[group])

    def remote(source, target, which, where):
        return pltpu.make_async_remote_copy(
            src_ref=source,
            dst_ref=target,
            send_sem=send_sems.at[which],
            recv_sem=recv_sems.at[which],
            device_id=where,
            device_id_type=MESH,
        )

    middle = 4 * ((fields // 4 + 1) // 2)
    halves = ((0, middle), (middle, fields))

    def in_halves(source, target, which, where):
        return [
            remote(
                source.at[pl.ds(a, b - a)], target.at[pl.ds(a, b - a)], which + i, where
            )
            for i, (a, b) in enumerate(halves)
        ]

    down = in_halves(to_partner, north, 0, {"lat": 1 - lat})
    across = in_halves(to_mirror, north, 2, {"lon": mirror})
    up = in_halves(to_partner, south, 4, {"lat": 1 - lat})

    padding = jnp.zeros((LANES - rows, cols), jnp.float32)
    for k in range(levels):
        for group, value in enumerate(fields_of(k, 0, rows)):
            whole = jnp.concatenate([value, padding], axis=0)
            ext[group * levels + k, DEPTH : DEPTH + cols, :] = whole.T

    ends = ((DEPTH, DEPTH + cols, west), (cols, 0, east))

    def strips(fields_ref, begin, count, first):
        return [
            remote(
                fields_ref.at[pl.ds(begin, count), pl.ds(source, DEPTH)],
                fields_ref.at[pl.ds(begin, count), pl.ds(target, DEPTH)],
                first + i,
                {"lon": where},
            )
            for i, (source, target, where) in enumerate(ends)
        ]

    sent = fields * 3 // 4

    def thirds():
        for i in range(sent):
            yield i, sent + i // 3, 32 * (i % 3)

    for start in (DEPTH, cols):
        for carrier, rider, at in thirds():
            piece = ext[rider, start : start + DEPTH, at : at + 32]
            ext[carrier, start : start + DEPTH, LANES - 32 :] = piece

    @pl.when(is_top)
    def _():
        pl.semaphore_wait(barrier, 4)
        for i in range(2):
            across[i].start()
            down[i].start()

    @pl.when(jnp.logical_not(is_top))
    def _():
        pl.semaphore_wait(barrier, 3)
        for i in range(2):
            up[i].start()
        south[...] = jnp.zeros_like(south)

    strip_sends = strips(ext, 0, sent, 6)
    rim_sends = [
        strips(rim, a // 4, (b - a) // 4, 8 + 2 * i) for i, (a, b) in enumerate(halves)
    ]
    for send in strip_sends:
        send.start()

    nothing = jnp.zeros((8, cols), jnp.float32)
    for half in range(2):

        @pl.when(is_top)
        def _():
            up[half].wait_recv()
            across[half].wait_recv()

        @pl.when(jnp.logical_not(is_top))
        def _():
            down[half].wait_recv()

        for first in range(*halves[half], 4):
            halo = []
            for index in range(first, first + 4):
                plain = north[index]
                halo += [
                    jnp.where(is_top, pltpu.roll(plain, 1, 1), plain),
                    jnp.where(is_top, plain, 0.0),
                    nothing,
                    south[index],
                ]
            rim[first // 4, DEPTH : DEPTH + cols, :] = jnp.concatenate(halo, axis=0).T
        for send in rim_sends[half]:
            send.start()
    for send in strip_sends:
        send.wait()

    def merge(start, stop):
        for index in range(fields):
            at = 32 * (index % 4)
            ext[index, start:stop, LANES - 32 :] = rim[index // 4, start:stop, at : at + 32]

    for start in (0, DEPTH + cols):
        for carrier, rider, at in thirds():
            piece = ext[carrier, start : start + DEPTH, LANES - 32 :]
            ext[rider, start : start + DEPTH, at : at + 32] = piece
    merge(DEPTH, DEPTH + cols)

    def place(start, stop):
        lanes = lax.broadcasted_iota(jnp.int32, (stop - start, LANES), 1)
        inside = jnp.logical_or(lanes < rows + 8, lanes >= LANES - 8)
        for k in range(levels):
            for d, (shift_lat, _) in enumerate(OFFSETS):
                value = jnp.where(inside, ext[d * levels + k, start:stop, :], 0.0)
                if shift_lat:
                    value = pltpu.roll(value, shift_lat % LANES, 1)
                weights[d * levels + k, start:stop, :] = value

    place(2 * DEPTH, DEPTH + cols)
    for send in rim_sends[0] + rim_sends[1]:
        send.wait()
    merge(0, DEPTH)
    merge(DEPTH + cols, total)

    lane_row = lax.broadcasted_iota(jnp.int32, (fields, LANES), 1)
    ghost = jnp.logical_and(jnp.logical_and(lane_row >= rows, lane_row < rows + 8), is_top)
    for seam in (DEPTH, DEPTH + cols):
        before = pltpu.roll(ext[:, seam - 1, :], LANES - 8, 1)
        ext[:, seam, :] = jnp.where(ghost, before, ext[:, seam, :])
    place(0, 2 * DEPTH)
    place(DEPTH + cols, total)

    chunks = total // 8
    sub_all = lax.broadcasted_iota(jnp.int32, (8, LANES), 0)
    low, high = sub_all == 0, sub_all == 7

    def parts(k, s):
        at = pl.ds(8 * s, 8)
        u = update[k, at, :]
        by_lat = {0: u, 1: pltpu.roll(u, 1, 1), -1: pltpu.roll(u, LANES - 1, 1)}
        sums = {}
        for d, (shift_lat, shift_lon) in enumerate(OFFSETS):
            term = weights[d * levels + k, at, :] * by_lat[shift_lat]
            sums[shift_lon] = sums[shift_lon] + term if shift_lon in sums else term
        return sums[-1], sums[0], sums[1], u

    def sweep(keep_ratio, gain):
        held = [[None] * chunks for _ in range(levels)]
        for s in range(chunks + 1):
            for k in range(levels):
                if s < chunks:
                    held[k][s] = parts(k, s)
                if s == 0:
                    continue
                t = s - 1
                here = held[k][t]
                left = held[k][t - 1][2] if t else here[2]
                right = held[k][s][0] if s < chunks else here[0]
                gained = (
                    here[1]
                    + pltpu.roll(jnp.where(high, left, here[2]), 1, 0)
                    + pltpu.roll(jnp.where(low, right, here[0]), 7, 0)
                )
                at = pl.ds(8 * t, 8)
                res = (residual[k, at, :] - here[3]) + gained
                new = keep_ratio * here[3] + gain * res
                residual[k, at, :] = res
                update[k, at, :] = new
                iterate[k, at, :] = iterate[k, at, :] + new

    sigma_ratio = CENTRE_VALUE / HALF_WIDTH
    ratio_now = 1.0 / sigma_ratio
    factors = []
    for _ in range(ITERS):
        ratio_next = 1.0 / (2.0 * sigma_ratio - ratio_now)
        factors.append((ratio_next * ratio_now, 2.0 * ratio_next / HALF_WIDTH))
        ratio_now = ratio_next

    def pick(values, i):
        chosen = jnp.float32(values[-1])
        for n in range(len(values) - 1):
            chosen = jnp.where(i == n, jnp.float32(values[n]), chosen)
        return chosen

    for step in range(STEPS):
        for k in range(levels):
            start = ext[z_at + k] if step == 0 else ext[pm_at + k] * iterate[k]
            residual[k] = start
            first = start * (1.0 / CENTRE_VALUE)
            update[k] = first
            iterate[k] = first

        @pl.loop(0, ITERS)
        def _(i):
            sweep(pick([f[0] for f in factors], i), pick([f[1] for f in factors], i))

    for k in range(levels):
        own = (ext[pm_at + k, DEPTH : DEPTH + cols] * iterate[k, DEPTH : DEPTH + cols]).T
        out[k] = own[:rows]

    @pl.when(is_top)
    def _():
        for i in range(2):
            down[i].wait_send()
            across[i].wait_send()

    @pl.when(jnp.logical_not(is_top))
    def _():
        for i in range(2):
            up[i].wait_send()


def body(n_lon, forcing, coeffs, sea_mask, fold_pair, norm_scale):
    levels, rows, cols = forcing.shape
    fields = 10 * levels
    total = cols + 2 * DEPTH
    edge = pltpu.VMEM((fields, 8, cols), jnp.float32)
    tile = pltpu.VMEM(forcing.shape, jnp.float32)
    field = pltpu.VMEM((levels, total, LANES), jnp.float32)
    return pl.pallas_call(
        functools.partial(kernel, n_lon),
        out_shape=jax.ShapeDtypeStruct(forcing.shape, jnp.float32),
        in_specs=[pl.BlockSpec(memory_space=pltpu.HBM)] * 5,
        out_specs=pl.BlockSpec(memory_space=pltpu.VMEM),
        scratch_shapes=[
            tile,
            pltpu.VMEM(coeffs.shape, jnp.float32),
            pltpu.VMEM(sea_mask.shape, jnp.int32),
            pltpu.VMEM((n_lon, cols), jnp.int32),
            tile,
            edge,
            edge,
            edge,
            edge,
            pltpu.VMEM((fields, total, LANES), jnp.float32),
            pltpu.VMEM((fields // 4, total, LANES), jnp.float32),
            pltpu.VMEM((8 * levels, total, LANES), jnp.float32),
            field,
            field,
            field,
            pltpu.SemaphoreType.DMA((5,)),
            pltpu.SemaphoreType.DMA((12,)),
            pltpu.SemaphoreType.DMA((12,)),
        ],
        compiler_params=pltpu.CompilerParams(
            collective_id=0, has_side_effects=True, vmem_limit_bytes=60 * 1024 * 1024
        ),
    )(forcing, coeffs, sea_mask, fold_pair.reshape(n_lon, cols), norm_scale) * norm_scale


def solution(mesh):
    placed = (
        P("member", "lat", "lon"),
        P(None, None, "lat", "lon"),
        P(None, "lat", "lon"),
        P(),
        P(None, "lat", "lon"),
    )
    return jax.shard_map(
        functools.partial(body, mesh.shape["lon"]),
        mesh=mesh,
        in_specs=placed,
        out_specs=P("member", "lat", "lon"),
        check_vma=False,
    )
```
